128 devices in a mesh: pole: 4 (over y_lo, core), dom: 32 (over z, x, y_hi).
Axes of the slice: x: 4, y: 4 (y_hi: 2, y_lo: 2; y = y_hi * 2 + y_lo), z: 4, core: 2. Of those that a mesh axis runs over, the one named last changes fastest.
Arguments:
- initial_block: bfloat16 [32, 8, 512, 256], P('dom'), may hold values from -24 to 24
- coupling: bfloat16 [32, 8, 512, 512], P('dom'), may hold values from -0.125 to 0.125
- pivots: bfloat16 [4, 32, 8, 2, 512, 512], P('pole', 'dom'), may hold values from -0.125 to 0.125
- interface: bfloat16 [4, 32, 3, 2, 512, 512], P('pole', 'dom'), may hold values from -0.1875 to 0.1875
- pole_values: float32 [4, 4], P('pole'), may hold values from 0.5 to 1.5
Outputs:
- filtered_basis: float32 [32, 8, 512, 256], P('dom', 'pole')
- rayleigh: float32 [256, 256], replicated
The draws below stay inside these ranges and needn't reach their ends.
All inputs are finite; a program needn't handle non-finite values.
Results may differ from the reference program's by a relative error of at most 0.008.
Values sent between devices are 32-bit elements; how exact they have to be, the bound alone decides.
A program may use at most 192 MiB of HBM per device.

```python
import math
import jax
import jax.numpy as jnp
from jax import lax

B = 512
M = 256
PB = 8
PARTS_SIZE = 32
POLES = 4
ROWS = 131072


def draw_initial_block(key, part):
    noise_key = jax.random.fold_in(key, 11)
    scale_key = jax.random.fold_in(key, 23)
    base = jnp.clip(jax.random.normal(noise_key, (PARTS_SIZE, PB, B, M), jnp.float32), -6.0, 6.0)
    scales = jnp.exp(jax.random.uniform(scale_key, (PARTS_SIZE, PB, 1, 1), jnp.float32, 0.0, math.log(4.0)))
    return (base * scales).astype(jnp.bfloat16)


def shard_levels(own_key, dims, pieces, low, largest):
    factor_of, own = 1.0, jax.random.fold_in(own_key, 6)
    for axis_at, parts in pieces:
        steps = jnp.exp(jax.random.uniform(jax.random.fold_in(own, axis_at), (parts,), jnp.float32, low / len(pieces), largest / len(pieces)))
        factor_of = factor_of * jnp.repeat(steps, dims[axis_at] // parts).reshape([-1 if axis == axis_at else 1 for axis in range(len(dims))])
    return factor_of


def noise(key, extent, deviation, reach, cuts=(), kind=jnp.bfloat16):
    level = shard_levels(key, extent, cuts, -0.22, 0.18) if cuts else 1.0
    values = jax.random.normal(key, extent, jnp.float32) * deviation * level
    return jnp.minimum(jnp.maximum(values, -reach), reach).astype(kind)


def setup_inputs(seed: int = 0) -> dict:
    key_list = jax.random.split(jax.random.key(seed), 6)
    initial_block = draw_initial_block(jax.random.fold_in(key_list[5], 71), 0)
    coupling = noise(key_list[1], (PARTS_SIZE, PB, B, B), (4 * B) ** -0.5, 0.125, ((0, 32),))
    pivots = noise(key_list[2], (POLES, PARTS_SIZE, PB, 2, B, B), (4 * B) ** -0.5, 0.125, ((0, 4), (1, 32)))
    interface = noise(key_list[3], (POLES, PARTS_SIZE, 3, 2, B, B), (2 * B) ** -0.5, 0.1875, ((0, 4), (1, 32)))
    pole_values = jnp.clip(0.5 + 1.0 * jax.random.uniform(key_list[4], (POLES, 4), jnp.float32) ** shard_levels(key_list[4], (POLES, 4), ((0, 4),), -0.2, 0.2), 0.5, 1.5)
    return dict(initial_block=initial_block, coupling=coupling, pivots=pivots, interface=interface, pole_values=pole_values)


def lower_solve(factor, right_side):
    return lax.linalg.triangular_solve(factor, right_side, left_side=True, lower=True)

def complex_product(matrix, vectors):
    block_order = matrix.shape[1]
    half_width = vectors.shape[1] // 2
    stacked = matrix.reshape(2 * block_order, block_order)
    stacked_out = jnp.dot(stacked.astype(jnp.float32), vectors.astype(jnp.bfloat16).astype(jnp.float32), preferred_element_type=jnp.float32)
    real_part = stacked_out[:block_order, :half_width] - stacked_out[block_order:, half_width:]
    imag_part = stacked_out[:block_order, half_width:] + stacked_out[block_order:, :half_width]
    return jnp.concatenate([real_part, imag_part], axis=1)

def real_product(matrix, vectors):
    return jnp.dot(matrix.astype(jnp.float32), vectors.astype(jnp.bfloat16).astype(jnp.float32), preferred_element_type=jnp.float32)

def transposed_product(matrix, vectors):
    return lax.dot_general(matrix.astype(jnp.float32), vectors.astype(jnp.bfloat16).astype(jnp.float32), (((0,), (0,)), ((), ())), preferred_element_type=jnp.float32)

def inner_products(left, right_side):
    return lax.dot_general(left.astype(jnp.float32), right_side.astype(jnp.float32), (((0,), (0,)), ((), ())), precision=lax.Precision.HIGHEST, preferred_element_type=jnp.float32)

def partition_solve(inverse, coupled, source):
    previous = jnp.roll(coupled, 1, axis=0)
    initial = jnp.zeros(source.shape[1:], jnp.float32)

    def forward_step(carried, members):
        block_inverse, given, couple_prev = members
        result = complex_product(block_inverse, given + transposed_product(couple_prev, carried))
        return (result, result)
    unused, forward = lax.scan(forward_step, initial, (inverse, source, previous))

    def backward_step(carried, members):
        block_inverse, partial_value, couple_next = members
        result = partial_value + complex_product(block_inverse, real_product(couple_next, carried))
        return (result, result)
    unused, backward = lax.scan(backward_step, initial, (inverse, forward, coupled), reverse=True)
    return backward

def reference(initial_block, coupling, pivots, interface, pole_values):
    real_start = initial_block.astype(jnp.float32)
    source = jnp.concatenate([real_start, jnp.zeros_like(real_start)], axis=-1)
    basis_sum = jnp.zeros(real_start.shape, jnp.float32)
    shifted_sum = jnp.zeros(real_start.shape, jnp.float32)
    links = coupling[:, PB - 1]
    for pole_index in range(POLES):
        inverse = pivots[pole_index]
        first = jax.vmap(partition_solve)(inverse, coupling, source)
        bottom = first[:, PB - 1]
        top = first[:, 0]
        top_next = jnp.concatenate([top[1:], jnp.zeros_like(top[:1])], axis=0)
        factors = interface[pole_index]
        below = jax.vmap(complex_product)(factors[:, 0], bottom) - jax.vmap(complex_product)(factors[:, 1], top_next)
        above = top_next - jax.vmap(complex_product)(factors[:, 2], below)
        above = above.at[PARTS_SIZE - 1].set(0.0)
        lifted = jax.vmap(transposed_product)(links, below)
        arriving = jnp.concatenate([jnp.zeros_like(lifted[:1]), lifted[:-1]], axis=0)
        update = source.at[:, 0].add(arriving)
        update = update.at[:, PB - 1].add(jax.vmap(real_product)(links, above))
        second = jax.vmap(partition_solve)(inverse, coupling, update)
        real_z = pole_values[pole_index, 0]
        imag_z = pole_values[pole_index, 1]
        real_w = pole_values[pole_index, 2]
        imag_w = pole_values[pole_index, 3]
        real_x = second[..., :M]
        imag_x = second[..., M:]
        basis_sum = basis_sum + (real_w * real_x - imag_w * imag_x)
        shifted_sum = shifted_sum + ((real_w * real_z - imag_w * imag_z) * real_x - (real_w * imag_z + imag_w * real_z) * imag_x - real_w * real_start)
    flat = basis_sum.reshape(ROWS, M)
    shifted = shifted_sum.reshape(ROWS, M)
    gram = inner_products(flat, flat) / ROWS
    projected = inner_products(flat, shifted) / ROWS
    factor = jnp.linalg.cholesky(gram)
    filtered_basis = lower_solve(factor, flat.T).T.reshape(PARTS_SIZE, PB, B, M)
    middle = lower_solve(factor, projected)
    rayleigh = lower_solve(factor, middle.T).T
    return (filtered_basis, rayleigh)
```

```python
import jax
import jax.numpy as jnp
from jax import lax
from jax.experimental import pallas as pl
from jax.experimental.pallas import tpu as pltpu
from jax.sharding import PartitionSpec as P

B = 512
M = 256
H = M // 2
PB = 8
PARTS = 32
F32 = jnp.float32
BF16 = jnp.bfloat16
MESH = pl.DeviceIdType.MESH


def dot_nn(left, right):
    return jnp.dot(left, right, preferred_element_type=F32)


def dot_nt(left, right):
    return lax.dot_general(left, right, (((1,), (1,)), ((), ())), preferred_element_type=F32)


def complex_rows(rows, matrix):
    out = dot_nt(rows.astype(BF16), matrix)
    real_part = out[:H, :B] - out[H:, B:]
    imag_part = out[H:, :B] + out[:H, B:]
    return jnp.concatenate([real_part, imag_part], axis=0)


def filter_kernel(
    f_hbm, u_hbm, g_hbm, i_hbm, pole_ref, y_ref, z_ref,
    f_raw, f_rows, u_mat, g_mat, i_mat, work, first_s, lifted_d,
    t_send, t_recv, c_send, c_recv, terms, core_recv, far_recv,
    f_sem, u_sem, g_sem, i_sem, t_ss, t_rs, c_ss, c_rs, q_ss, q_rs, y_ss, y_rs,
):
    pole = lax.axis_index("pole")
    dom = lax.axis_index("dom")
    core = lax.rem(pole, 2)
    side = pole // 2
    upper = lax.rem(dom + PARTS - 1, PARTS)
    lower = lax.rem(dom + 1, PARTS)
    core_mate = (2 * side + 1 - core, dom)
    side_mate = (2 * (1 - side) + core, dom)

    loads = []
    for k in range(PB):
        loads.append(
            (
                pltpu.make_async_copy(f_hbm.at[k], f_raw.at[k], f_sem.at[k]),
                pltpu.make_async_copy(g_hbm.at[k], g_mat.at[k], g_sem.at[k]),
                pltpu.make_async_copy(u_hbm.at[k], u_mat.at[k], u_sem.at[k]),
            )
        )
        for copy in loads[-1]:
            copy.start()
    interface_load = pltpu.make_async_copy(i_hbm, i_mat, i_sem)
    interface_load.start()

    barrier = pltpu.get_barrier_semaphore()
    for mate in (core_mate, side_mate, (pole, upper), (pole, lower)):
        pl.semaphore_signal(barrier, inc=1, device_id=mate, device_id_type=MESH)

    real_z = pole_ref[0, 0]
    imag_z = pole_ref[0, 1]
    real_w = pole_ref[0, 2]
    imag_w = pole_ref[0, 3]
    real_wz = real_w * real_z - imag_w * imag_z
    imag_wz = real_w * imag_z + imag_w * real_z

    def f_half(k, half):
        return f_rows[k, half * H : (half + 1) * H, :].astype(F32)

    def wait_load(k):
        pltpu.make_async_copy(f_hbm.at[k], f_raw.at[k], f_sem.at[k]).wait()
        pltpu.make_async_copy(g_hbm.at[k], g_mat.at[k], g_sem.at[k]).wait()
        f_rows[k] = f_raw[k].T

    def wait_coupling(k):
        pltpu.make_async_copy(u_hbm.at[k], u_mat.at[k], u_sem.at[k]).wait()

    def forward_step(k, half, loading):
        if loading:
            wait_load(k)
            wait_coupling(k - 1)
        lifted = dot_nn(work[k - 1].astype(BF16), u_mat[k - 1])
        rows = jnp.concatenate([lifted[:H] + f_half(k, half), lifted[H:]], axis=0)
        return rows

    def first_solve(half):
        loading = half == 0
        if loading:
            wait_load(0)
        out = dot_nt(f_rows[0, half * H : (half + 1) * H, :], g_mat[0])
        work[0] = jnp.concatenate([out[:, :B], out[:, B:]], axis=0)

        def forward(k, carry):
            work[k] = complex_rows(forward_step(k, half, loading), g_mat[k])
            return carry

        lax.fori_loop(1, PB, forward, 0)

        def backward(i, carry):
            k = PB - 2 - i
            lifted = dot_nt(work[k + 1].astype(BF16), u_mat[k])
            work[k] = work[k] + complex_rows(lifted, g_mat[k])
            return carry

        lax.fori_loop(0, PB - 1, backward, 0)
        t_send[half] = work[0]

    def t_copy(half):
        return pltpu.make_async_remote_copy(
            src_ref=t_send.at[half], dst_ref=t_recv.at[half],
            send_sem=t_ss.at[half], recv_sem=t_rs.at[half],
            device_id=(pole, upper), device_id_type=MESH,
        )

    def c_copy(half):
        return pltpu.make_async_remote_copy(
            src_ref=c_send.at[half], dst_ref=c_recv.at[half],
            send_sem=c_ss.at[half], recv_sem=c_rs.at[half],
            device_id=(pole, lower), device_id_type=MESH,
        )

    def core_copy(half, quad):
        start = 4 * quad + 2 * (1 - core)
        return pltpu.make_async_remote_copy(
            src_ref=terms.at[half, pl.ds(start, 2)], dst_ref=core_recv.at[half, quad],
            send_sem=q_ss.at[half, quad], recv_sem=q_rs.at[half, quad],
            device_id=core_mate, device_id_type=MESH,
        )

    def far_copy(half, quad):
        return pltpu.make_async_remote_copy(
            src_ref=core_recv.at[half, quad], dst_ref=far_recv.at[half],
            send_sem=y_ss.at[half], recv_sem=y_rs.at[half],
            device_id=side_mate, device_id_type=MESH,
        )

    def interface(half):
        last = dom == PARTS - 1
        t_next = jnp.where(last, 0.0, t_recv[half])
        below = first_s[half] - complex_rows(t_next, i_mat[1])
        c_send[half] = dot_nn(below.astype(BF16), u_mat[PB - 1])
        c_copy(half).start()
        above = jnp.where(last, 0.0, t_next - complex_rows(below, i_mat[2]))
        lifted_d[half] = dot_nt(above.astype(BF16), u_mat[PB - 1])

    def emit_terms(k, half):
        real_x = work[k, :H]
        imag_x = work[k, H:]
        terms[half, k, 0] = real_w * real_x - imag_w * imag_x
        terms[half, k, 1] = (
            real_wz * real_x - imag_wz * imag_x - real_w * f_half(k, half)
        )

    def second_solve(half):
        arrived = jnp.where(dom == 0, 0.0, c_recv[half])
        rows = jnp.concatenate([arrived[:H] + f_half(0, half), arrived[H:]], axis=0)
        work[0] = complex_rows(rows, g_mat[0])

        def forward(k, carry):
            work[k] = complex_rows(forward_step(k, half, False), g_mat[k])
            return carry

        lax.fori_loop(1, PB - 1, forward, 0)
        rows = forward_step(PB - 1, half, False) + lifted_d[half]
        work[PB - 1] = complex_rows(rows, g_mat[PB - 1])
        emit_terms(PB - 1, half)

        def backward(i, carry):
            k = PB - 2 - i
            lifted = dot_nt(work[k + 1].astype(BF16), u_mat[k])
            work[k] = work[k] + complex_rows(lifted, g_mat[k])
            emit_terms(k, half)
            return carry

        lax.fori_loop(0, 3, backward, 0)
        core_copy(half, 1).start()
        lax.fori_loop(3, PB - 1, backward, 0)
        core_copy(half, 0).start()

        for quad in (1, 0):
            core_copy(half, quad).wait()
            for i in range(2):
                core_recv[half, quad, i] += terms[half, 4 * quad + 2 * core + i]

            @pl.when(side == 1 - quad)
            def _():
                far_copy(half, quad).start()

    first_solve(0)
    pl.semaphore_wait(barrier, 4)
    t_copy(0).start()
    interface_load.wait()
    wait_coupling(PB - 1)
    first_s[0] = complex_rows(work[PB - 1], i_mat[0])
    first_solve(1)
    t_copy(1).start()
    first_s[1] = complex_rows(work[PB - 1], i_mat[0])
    for half in range(2):
        t_copy(half).wait()
        interface(half)
    for half in range(2):
        c_copy(half).wait()
        second_solve(half)
    for half in range(2):
        far_copy(half, 0).wait()
        for i in range(2):
            y_ref[i, half * H : (half + 1) * H, :] = core_recv[half, side, i, 0] + far_recv[half, i, 0]
            z_ref[i, half * H : (half + 1) * H, :] = core_recv[half, side, i, 1] + far_recv[half, i, 1]


def filtered_sums(f, u, g, interface, pole_values):
    own = jax.ShapeDtypeStruct((2, M, B), F32)
    dma = pltpu.SemaphoreType.DMA
    return pl.pallas_call(
        filter_kernel,
        out_shape=(own, own),
        in_specs=[pl.BlockSpec(memory_space=pl.ANY)] * 4 + [pl.BlockSpec(memory_space=pltpu.SMEM)],
        out_specs=(pl.BlockSpec(memory_space=pltpu.VMEM), pl.BlockSpec(memory_space=pltpu.VMEM)),
        scratch_shapes=[
            pltpu.VMEM((PB, B, M), BF16),
            pltpu.VMEM((PB, M, B), BF16),
            pltpu.VMEM((PB, B, B), BF16),
            pltpu.VMEM((PB, 2 * B, B), BF16),
            pltpu.VMEM((3, 2 * B, B), BF16),
            pltpu.VMEM((PB, M, B), F32),
            pltpu.VMEM((2, M, B), F32),
            pltpu.VMEM((2, M, B), F32),
            pltpu.VMEM((2, M, B), F32),
            pltpu.VMEM((2, M, B), F32),
            pltpu.VMEM((2, M, B), F32),
            pltpu.VMEM((2, M, B), F32),
            pltpu.VMEM((2, PB, 2, H, B), F32),
            pltpu.VMEM((2, 2, 2, 2, H, B), F32),
            pltpu.VMEM((2, 2, 2, H, B), F32),
            dma((PB,)), dma((PB,)), dma((PB,)), dma,
            dma((2,)), dma((2,)), dma((2,)), dma((2,)),
            dma((2, 2)), dma((2, 2)), dma((2,)), dma((2,)),
        ],
        compiler_params=pltpu.CompilerParams(
            collective_id=0, has_side_effects=True, vmem_limit_bytes=60 * 2**20
        ),
        name="filter_sums",
    )(f, u, g, interface, pole_values)


def lower_solve(factor, right_side):
    return lax.linalg.triangular_solve(factor, right_side, left_side=True, lower=True)


def row_products(left, right):
    return jnp.einsum(
        "bvk,bwk->vw", left, right,
        precision=lax.Precision.HIGHEST, preferred_element_type=F32,
    )


def on_device(initial_block, coupling, pivots, interface, pole_values):
    y_rows, z_rows = filtered_sums(
        initial_block[0],
        coupling[0],
        pivots[0, 0].reshape(PB, 2 * B, B),
        interface[0, 0].reshape(3, 2 * B, B),
        pole_values,
    )
    gram_part = row_products(y_rows, y_rows)
    projected_part = row_products(y_rows, z_rows)
    gram_total, projected_total = lax.psum((gram_part, projected_part), ("pole", "dom"))
    row_total = PB * B * PARTS
    gram = gram_total / row_total
    projected = projected_total / row_total
    factor = jnp.linalg.cholesky(gram)
    inverse = lower_solve(factor, jnp.eye(M, dtype=F32))
    filtered_basis = jnp.einsum(
        "bvk,wv->bkw", y_rows, inverse,
        precision=lax.Precision.HIGHEST, preferred_element_type=F32,
    )[None]
    middle = jnp.dot(inverse, projected, precision=lax.Precision.HIGHEST)
    rayleigh = lax.dot_general(
        middle, inverse, (((1,), (1,)), ((), ())), precision=lax.Precision.HIGHEST
    )
    return (filtered_basis, rayleigh)


def solution(mesh):
    in_specs = (
        P("dom", None, None, None),
        P("dom", None, None, None),
        P("pole", "dom", None, None, None, None),
        P("pole", "dom", None, None, None, None),
        P("pole", None),
    )
    out_specs = (P("dom", "pole", None, None), P())
    return jax.shard_map(
        on_device, mesh=mesh, in_specs=in_specs, out_specs=out_specs, check_vma=False
    )
```

```python
import jax
import jax.numpy as jnp
from jax import lax
from jax.experimental import pallas as pl
from jax.experimental.pallas import tpu as pltpu
from jax.sharding import PartitionSpec as P

B = 512
M = 256
H = M // 2
PB = 8
PARTS = 32
F32 = jnp.float32
BF16 = jnp.bfloat16
MESH = pl.DeviceIdType.MESH
HIGHEST = lax.Precision.HIGHEST
MATES = 2 * PARTS
PIECE = 2 * M // MATES
NB = 64


def dot_nn(left, right):
    return jnp.dot(left, right, preferred_element_type=F32)


def dot_nt(left, right):
    return lax.dot_general(left, right, (((1,), (1,)), ((), ())), preferred_element_type=F32)


def exact_dot(left, right, left_dim, right_dim):
    return lax.dot_general(
        left, right, (((left_dim,), (right_dim,)), ((), ())),
        precision=HIGHEST, preferred_element_type=F32,
    )


def complex_rows(rows, matrix):
    out = dot_nt(rows.astype(BF16), matrix)
    real_part = out[:H, :B] - out[H:, B:]
    imag_part = out[H:, :B] + out[:H, B:]
    return jnp.concatenate([real_part, imag_part], axis=0)


def filter_kernel(
    f_hbm, u_hbm, g_hbm, i_hbm, pole_ref, y_ref, sum_ref,
    f_raw, f_rows, u_mat, g_mat, i_mat, work, first_s, lifted_d,
    t_send, t_recv, c_send, c_recv, terms, core_recv, far_recv,
    z_own, parts, core_part, mine, pieces,
    f_sem, u_sem, g_sem, i_sem, t_ss, t_rs, c_ss, c_rs, q_ss, q_rs, y_ss, y_rs, a_ss, a_rs,
):
    pole = lax.axis_index("pole")
    dom = lax.axis_index("dom")
    core = lax.rem(pole, 2)
    side = pole // 2
    upper = lax.rem(dom + PARTS - 1, PARTS)
    lower = lax.rem(dom + 1, PARTS)
    core_mate = (2 * side + 1 - core, dom)
    side_mate = (2 * (1 - side) + core, dom)

    loads = []
    for k in range(PB):
        loads.append(
            (
                pltpu.make_async_copy(f_hbm.at[k], f_raw.at[k], f_sem.at[k]),
                pltpu.make_async_copy(g_hbm.at[k], g_mat.at[k], g_sem.at[k]),
                pltpu.make_async_copy(u_hbm.at[k], u_mat.at[k], u_sem.at[k]),
            )
        )
        for copy in loads[-1]:
            copy.start()
    interface_load = pltpu.make_async_copy(i_hbm, i_mat, i_sem)
    interface_load.start()

    barrier = pltpu.get_barrier_semaphore()
    place = side * PARTS + dom

    def mate_of(step):
        other = lax.rem(place + step, MATES)
        return other, (2 * (other // PARTS) + core, lax.rem(other, PARTS))

    pl.semaphore_signal(barrier, inc=1, device_id=core_mate, device_id_type=MESH)

    def greet(step, carry):
        pl.semaphore_signal(barrier, inc=1, device_id=mate_of(step)[1], device_id_type=MESH)
        return carry

    lax.fori_loop(1, MATES, greet, 0)

    real_z = pole_ref[0, 0]
    imag_z = pole_ref[0, 1]
    real_w = pole_ref[0, 2]
    imag_w = pole_ref[0, 3]
    real_wz = real_w * real_z - imag_w * imag_z
    imag_wz = real_w * imag_z + imag_w * real_z

    def f_half(k, half):
        return f_rows[k, half * H : (half + 1) * H, :].astype(F32)

    def wait_load(k):
        pltpu.make_async_copy(f_hbm.at[k], f_raw.at[k], f_sem.at[k]).wait()
        pltpu.make_async_copy(g_hbm.at[k], g_mat.at[k], g_sem.at[k]).wait()
        f_rows[k] = f_raw[k].T

    def wait_coupling(k):
        pltpu.make_async_copy(u_hbm.at[k], u_mat.at[k], u_sem.at[k]).wait()

    def forward_step(k, half, loading):
        if loading:
            wait_load(k)
            wait_coupling(k - 1)
        lifted = dot_nn(work[k - 1].astype(BF16), u_mat[k - 1])
        rows = jnp.concatenate([lifted[:H] + f_half(k, half), lifted[H:]], axis=0)
        return rows

    def first_solve(half):
        loading = half == 0
        if loading:
            wait_load(0)
        out = dot_nt(f_rows[0, half * H : (half + 1) * H, :], g_mat[0])
        work[0] = jnp.concatenate([out[:, :B], out[:, B:]], axis=0)

        def forward(k, carry):
            work[k] = complex_rows(forward_step(k, half, loading), g_mat[k])
            return carry

        lax.fori_loop(1, PB, forward, 0)

        def backward(i, carry):
            k = PB - 2 - i
            lifted = dot_nt(work[k + 1].astype(BF16), u_mat[k])
            work[k] = work[k] + complex_rows(lifted, g_mat[k])
            return carry

        lax.fori_loop(0, PB - 1, backward, 0)
        t_send[half] = work[0]

    def t_copy(half):
        return pltpu.make_async_remote_copy(
            src_ref=t_send.at[half], dst_ref=t_recv.at[half],
            send_sem=t_ss.at[half], recv_sem=t_rs.at[half],
            device_id=(pole, upper), device_id_type=MESH,
        )

    def c_copy(half):
        return pltpu.make_async_remote_copy(
            src_ref=c_send.at[half], dst_ref=c_recv.at[half],
            send_sem=c_ss.at[half], recv_sem=c_rs.at[half],
            device_id=(pole, lower), device_id_type=MESH,
        )

    def core_copy(half, quad):
        start = 4 * quad + 2 * (1 - core)
        return pltpu.make_async_remote_copy(
            src_ref=terms.at[half, pl.ds(start, 2)], dst_ref=core_recv.at[half, quad],
            send_sem=q_ss.at[half, quad], recv_sem=q_rs.at[half, quad],
            device_id=core_mate, device_id_type=MESH,
        )

    def far_copy(half, quad):
        return pltpu.make_async_remote_copy(
            src_ref=core_recv.at[half, quad], dst_ref=far_recv.at[half],
            send_sem=y_ss.at[half], recv_sem=y_rs.at[half],
            device_id=side_mate, device_id_type=MESH,
        )

    def interface(half):
        last = dom == PARTS - 1
        t_next = jnp.where(last, 0.0, t_recv[half])
        below = first_s[half] - complex_rows(t_next, i_mat[1])
        c_send[half] = dot_nn(below.astype(BF16), u_mat[PB - 1])
        c_copy(half).start()
        above = jnp.where(last, 0.0, t_next - complex_rows(below, i_mat[2]))
        lifted_d[half] = dot_nt(above.astype(BF16), u_mat[PB - 1])

    def emit_terms(k, half):
        real_x = work[k, :H]
        imag_x = work[k, H:]
        terms[half, k, 0] = real_w * real_x - imag_w * imag_x
        terms[half, k, 1] = (
            real_wz * real_x - imag_wz * imag_x - real_w * f_half(k, half)
        )

    def second_solve(half):
        arrived = jnp.where(dom == 0, 0.0, c_recv[half])
        rows = jnp.concatenate([arrived[:H] + f_half(0, half), arrived[H:]], axis=0)
        work[0] = complex_rows(rows, g_mat[0])

        def forward(k, carry):
            work[k] = complex_rows(forward_step(k, half, False), g_mat[k])
            return carry

        lax.fori_loop(1, PB - 1, forward, 0)
        rows = forward_step(PB - 1, half, False) + lifted_d[half]
        work[PB - 1] = complex_rows(rows, g_mat[PB - 1])
        emit_terms(PB - 1, half)

        def backward(i, carry):
            k = PB - 2 - i
            lifted = dot_nt(work[k + 1].astype(BF16), u_mat[k])
            work[k] = work[k] + complex_rows(lifted, g_mat[k])
            emit_terms(k, half)
            return carry

        lax.fori_loop(0, 3, backward, 0)
        core_copy(half, 1).start()
        lax.fori_loop(3, PB - 1, backward, 0)
        core_copy(half, 0).start()

        for quad in (1, 0):
            core_copy(half, quad).wait()
            for i in range(2):
                core_recv[half, quad, i] += terms[half, 4 * quad + 2 * core + i]

            @pl.when(side == 1 - quad)
            def _():
                far_copy(half, quad).start()

    first_solve(0)
    pl.semaphore_wait(barrier, MATES)
    t_copy(0).start()
    interface_load.wait()
    wait_coupling(PB - 1)
    first_s[0] = complex_rows(work[PB - 1], i_mat[0])
    first_solve(1)
    t_copy(1).start()
    first_s[1] = complex_rows(work[PB - 1], i_mat[0])
    for half in range(2):
        t_copy(half).wait()
        interface(half)
    for half in range(2):
        c_copy(half).wait()
        second_solve(half)
    for half in range(2):
        far_copy(half, 0).wait()
        for i in range(2):
            y_ref[i, half * H : (half + 1) * H, :] = core_recv[half, side, i, 0] + far_recv[half, i, 0]
            z_own[i, half * H : (half + 1) * H, :] = core_recv[half, side, i, 1] + far_recv[half, i, 1]

    gram = exact_dot(y_ref[0], y_ref[0], 1, 1) + exact_dot(y_ref[1], y_ref[1], 1, 1)
    projected = exact_dot(y_ref[0], z_own[0], 1, 1) + exact_dot(y_ref[1], z_own[1], 1, 1)
    for i, part in enumerate((gram, projected)):
        parts[i, :M] = part[:, :H]
        parts[i, M:] = part[:, H:]

    def waited(ref, sem):
        pltpu.make_async_copy(ref, ref, sem).wait()

    swap = pltpu.make_async_remote_copy(
        src_ref=parts.at[1 - core], dst_ref=core_part, send_sem=a_ss.at[0], recv_sem=a_rs.at[0],
        device_id=core_mate, device_id_type=MESH,
    )
    swap.start()
    swap.wait()
    mine[...] = parts[core] + core_part[...]

    def scatter(step, carry):
        other, device = mate_of(step)
        pltpu.make_async_remote_copy(
            src_ref=mine.at[pl.ds(pl.multiple_of(other * PIECE, PIECE), PIECE)],
            dst_ref=pieces.at[step], send_sem=a_ss.at[1], recv_sem=a_rs.at[1],
            device_id=device, device_id_type=MESH,
        ).start()
        return carry

    lax.fori_loop(1, MATES, scatter, 0)
    own = pl.ds(pl.multiple_of(place * PIECE, PIECE), PIECE)
    waited(pieces.at[pl.ds(1, MATES - 1)], a_rs.at[1])
    waited(pieces.at[pl.ds(1, MATES - 1)], a_ss.at[1])
    pieces[0] = mine[own]
    sum_ref[core, own] = jnp.sum(pieces[...], axis=0) / (PARTS * PB * B)

    def gather(step, carry):
        pltpu.make_async_remote_copy(
            src_ref=sum_ref.at[core, own], dst_ref=sum_ref.at[core, own],
            send_sem=a_ss.at[2], recv_sem=a_rs.at[2],
            device_id=mate_of(step)[1], device_id_type=MESH,
        ).start()
        return carry

    lax.fori_loop(1, MATES, gather, 0)
    waited(pieces.at[pl.ds(1, MATES - 1)], a_rs.at[2])
    waited(pieces.at[pl.ds(1, MATES - 1)], a_ss.at[2])
    swap = pltpu.make_async_remote_copy(
        src_ref=sum_ref.at[core], dst_ref=sum_ref.at[core],
        send_sem=a_ss.at[3], recv_sem=a_rs.at[3],
        device_id=core_mate, device_id_type=MESH,
    )
    swap.start()
    swap.wait()


def filtered_sums(f, u, g, interface, pole_values):
    own = jax.ShapeDtypeStruct((2, M, B), F32)
    dma = pltpu.SemaphoreType.DMA
    return pl.pallas_call(
        filter_kernel,
        out_shape=(own, jax.ShapeDtypeStruct((2, 2 * M, H), F32)),
        in_specs=[pl.BlockSpec(memory_space=pl.ANY)] * 4 + [pl.BlockSpec(memory_space=pltpu.SMEM)],
        out_specs=(pl.BlockSpec(memory_space=pltpu.VMEM), pl.BlockSpec(memory_space=pltpu.VMEM)),
        scratch_shapes=[
            pltpu.VMEM((PB, B, M), BF16),
            pltpu.VMEM((PB, M, B), BF16),
            pltpu.VMEM((PB, B, B), BF16),
            pltpu.VMEM((PB, 2 * B, B), BF16),
            pltpu.VMEM((3, 2 * B, B), BF16),
            pltpu.VMEM((PB, M, B), F32),
            pltpu.VMEM((2, M, B), F32),
            pltpu.VMEM((2, M, B), F32),
            pltpu.VMEM((2, M, B), F32),
            pltpu.VMEM((2, M, B), F32),
            pltpu.VMEM((2, M, B), F32),
            pltpu.VMEM((2, M, B), F32),
            pltpu.VMEM((2, PB, 2, H, B), F32),
            pltpu.VMEM((2, 2, 2, 2, H, B), F32),
            pltpu.VMEM((2, 2, 2, H, B), F32),
            pltpu.VMEM((2, M, B), F32),
            pltpu.VMEM((2, 2 * M, H), F32),
            pltpu.VMEM((2 * M, H), F32),
            pltpu.VMEM((2 * M, H), F32),
            pltpu.VMEM((MATES, PIECE, H), F32),
            dma((PB,)), dma((PB,)), dma((PB,)), dma,
            dma((2,)), dma((2,)), dma((2,)), dma((2,)),
            dma((2, 2)), dma((2, 2)), dma((2,)), dma((2,)), dma((4,)), dma((4,)),
        ],
        compiler_params=pltpu.CompilerParams(
            collective_id=0, has_side_effects=True, vmem_limit_bytes=60 * 2**20
        ),
        name="filter_sums",
    )(f, u, g, interface, pole_values)


def factor_block(block, work, inverse):
    wide = (8, 2 * NB)
    row = lax.broadcasted_iota(jnp.int32, (NB, NB), 0)
    column = lax.broadcasted_iota(jnp.int32, (NB, NB), 1)
    work[...] = jnp.concatenate([block, jnp.where(row == column, 1.0, 0.0)], axis=1)
    place = lax.broadcasted_iota(jnp.int32, wide, 0)
    for first in range(0, NB, 8):
        rows = work[first : first + 8, :]
        spread = [
            jnp.broadcast_to(rows[:, first + j : first + j + 1], wide) for j in range(8)
        ]
        scales = jnp.zeros(wide, F32)
        for j in range(8):
            scale = 1.0 / jnp.broadcast_to(spread[j][j : j + 1], wide)
            scales = jnp.where(place == j, scale, scales)
            if j < 7:
                ratio = jnp.where(place > j, spread[j] * scale, 0.0)
                rows = rows - ratio * jnp.broadcast_to(rows[j : j + 1], wide)
                for i in range(j + 1, 8):
                    spread[i] = spread[i] - ratio * jnp.broadcast_to(spread[i][j : j + 1], wide)
        inverse[first : first + 8, :] = rows * jnp.sqrt(scales)
        if first + 8 < NB:
            change = exact_dot(rows * scales, rows, 0, 0)
            work[first + 8 :, :] = work[first + 8 :, :] - change[first + 8 : NB]


def basis_kernel(sum_ref, y_ref, basis_ref, rayleigh_ref, wide, work, block, inverse):
    row = lax.broadcasted_iota(jnp.int32, (M, M), 0)
    column = lax.broadcasted_iota(jnp.int32, (M, M), 1)
    wide[:, :H] = sum_ref[0, :M]
    wide[:, H:M] = sum_ref[0, M:]
    wide[:, M:] = jnp.where(row == column, 1.0, 0.0)
    for low in range(0, M, NB):
        high = low + NB
        factor_block(wide[low:high, low:high], work, block)
        reduced = exact_dot(block[:, NB:], wide[low:high, :], 1, 0)
        inverse[low:high, :] = reduced[:, M:]
        if high < M:
            change = exact_dot(reduced[:, :M], reduced, 0, 0)
            wide[high:, :] = wide[high:, :] - change[high:]
    projected = jnp.concatenate([sum_ref[1, :M], sum_ref[1, M:]], axis=1)
    middle = exact_dot(inverse[...], projected, 1, 0)
    rayleigh_ref[...] = exact_dot(middle, inverse[...], 1, 1)
    for i in range(2):
        basis_ref[i] = exact_dot(inverse[...], y_ref[i], 1, 0).T


def orthonormal_basis(sums, y_rows):
    return pl.pallas_call(
        basis_kernel,
        out_shape=(
            jax.ShapeDtypeStruct((2, B, M), F32),
            jax.ShapeDtypeStruct((M, M), F32),
        ),
        in_specs=[pl.BlockSpec(memory_space=pltpu.VMEM)] * 2,
        out_specs=(pl.BlockSpec(memory_space=pltpu.VMEM), pl.BlockSpec(memory_space=pltpu.VMEM)),
        scratch_shapes=[
            pltpu.VMEM((M, 2 * M), F32),
            pltpu.VMEM((NB, 2 * NB), F32),
            pltpu.VMEM((NB, 2 * NB), F32),
            pltpu.VMEM((M, M), F32),
        ],
        compiler_params=pltpu.CompilerParams(vmem_limit_bytes=32 * 2**20),
        name="orthonormal_basis",
    )(sums, y_rows)


def on_device(initial_block, coupling, pivots, interface, pole_values):
    y_rows, sums = filtered_sums(
        initial_block[0],
        coupling[0],
        pivots[0, 0].reshape(PB, 2 * B, B),
        interface[0, 0].reshape(3, 2 * B, B),
        pole_values,
    )
    basis, rayleigh = orthonormal_basis(sums, y_rows)
    return (basis[None], rayleigh)


def solution(mesh):
    in_specs = (
        P("dom", None, None, None),
        P("dom", None, None, None),
        P("pole", "dom", None, None, None, None),
        P("pole", "dom", None, None, None, None),
        P("pole", None),
    )
    out_specs = (P("dom", "pole", None, None), P())
    return jax.shard_map(
        on_device, mesh=mesh, in_specs=in_specs, out_specs=out_specs, check_vma=False
    )
```

```python
import jax
import jax.numpy as jnp
from jax import lax
from jax.experimental import pallas as pl
from jax.experimental.pallas import tpu as pltpu
from jax.sharding import PartitionSpec as P

B = 512
M = 256
H = M // 2
PB = 8
PARTS = 32
F32 = jnp.float32
BF16 = jnp.bfloat16
MESH = pl.DeviceIdType.MESH
HIGHEST = lax.Precision.HIGHEST
MATES = 2 * PARTS
PIECE = 2 * M // MATES
NB = 64
SPAN = 16


def dot_nn(left, right):
    return jnp.dot(left, right, preferred_element_type=F32)


def dot_nt(left, right):
    return lax.dot_general(left, right, (((1,), (1,)), ((), ())), preferred_element_type=F32)


def exact_dot(left, right, left_dim, right_dim):
    return lax.dot_general(
        left, right, (((left_dim,), (right_dim,)), ((), ())),
        precision=HIGHEST, preferred_element_type=F32,
    )


def complex_rows(rows, matrix):
    out = dot_nt(rows.astype(BF16), matrix)
    real_part = out[:H, :B] - out[H:, B:]
    imag_part = out[H:, :B] + out[:H, B:]
    return jnp.concatenate([real_part, imag_part], axis=0)


def filter_kernel(
    f_hbm, u_hbm, g_hbm, i_hbm, pole_ref, y_ref, sum_ref,
    f_raw, f_rows, u_mat, g_mat, i_mat, work, first_s, lifted_d,
    t_send, t_recv, c_send, c_recv, terms, core_recv, far_recv,
    z_own, parts, core_part, mine, pieces,
    f_sem, u_sem, g_sem, i_sem, t_ss, t_rs, c_ss, c_rs, q_ss, q_rs, y_ss, y_rs, a_ss, a_rs,
):
    pole = lax.axis_index("pole")
    dom = lax.axis_index("dom")
    core = lax.rem(pole, 2)
    side = pole // 2
    upper = lax.rem(dom + PARTS - 1, PARTS)
    lower = lax.rem(dom + 1, PARTS)
    core_mate = (2 * side + 1 - core, dom)
    side_mate = (2 * (1 - side) + core, dom)

    loads = []
    for k in range(PB):
        loads.append(
            (
                pltpu.make_async_copy(f_hbm.at[k], f_raw.at[k], f_sem.at[k]),
                pltpu.make_async_copy(g_hbm.at[k], g_mat.at[k], g_sem.at[k]),
                pltpu.make_async_copy(u_hbm.at[k], u_mat.at[k], u_sem.at[k]),
            )
        )
        for copy in loads[-1]:
            copy.start()
    interface_load = pltpu.make_async_copy(i_hbm, i_mat, i_sem)
    interface_load.start()

    barrier = pltpu.get_barrier_semaphore()
    place = side * PARTS + dom

    def mate_of(step):
        other = lax.rem(place + step, MATES)
        return other, (2 * (other // PARTS) + core, lax.rem(other, PARTS))

    pl.semaphore_signal(barrier, inc=1, device_id=core_mate, device_id_type=MESH)

    def greet(step, carry):
        pl.semaphore_signal(barrier, inc=1, device_id=mate_of(step)[1], device_id_type=MESH)
        return carry

    lax.fori_loop(1, MATES, greet, 0)

    real_z = pole_ref[0, 0]
    imag_z = pole_ref[0, 1]
    real_w = pole_ref[0, 2]
    imag_w = pole_ref[0, 3]
    real_wz = real_w * real_z - imag_w * imag_z
    imag_wz = real_w * imag_z + imag_w * real_z

    def f_half(k, half):
        return f_rows[k, half * H : (half + 1) * H, :].astype(F32)

    def wait_load(k):
        pltpu.make_async_copy(f_hbm.at[k], f_raw.at[k], f_sem.at[k]).wait()
        pltpu.make_async_copy(g_hbm.at[k], g_mat.at[k], g_sem.at[k]).wait()
        f_rows[k] = f_raw[k].T

    def wait_coupling(k):
        pltpu.make_async_copy(u_hbm.at[k], u_mat.at[k], u_sem.at[k]).wait()

    def forward_step(k, half, loading):
        if loading:
            wait_load(k)
            wait_coupling(k - 1)
        lifted = dot_nn(work[k - 1].astype(BF16), u_mat[k - 1])
        rows = jnp.concatenate([lifted[:H] + f_half(k, half), lifted[H:]], axis=0)
        return rows

    def first_solve(half):
        loading = half == 0
        if loading:
            wait_load(0)
        out = dot_nt(f_rows[0, half * H : (half + 1) * H, :], g_mat[0])
        work[0] = jnp.concatenate([out[:, :B], out[:, B:]], axis=0)

        def forward(k, carry):
            work[k] = complex_rows(forward_step(k, half, loading), g_mat[k])
            return carry

        lax.fori_loop(1, PB, forward, 0)

        def backward(i, carry):
            k = PB - 2 - i
            lifted = dot_nt(work[k + 1].astype(BF16), u_mat[k])
            work[k] = work[k] + complex_rows(lifted, g_mat[k])
            return carry

        lax.fori_loop(0, PB - 1, backward, 0)
        t_send[half] = work[0]

    def t_copy(half):
        return pltpu.make_async_remote_copy(
            src_ref=t_send.at[half], dst_ref=t_recv.at[half],
            send_sem=t_ss.at[half], recv_sem=t_rs.at[half],
            device_id=(pole, upper), device_id_type=MESH,
        )

    def c_copy(half):
        return pltpu.make_async_remote_copy(
            src_ref=c_send.at[half], dst_ref=c_recv.at[half],
            send_sem=c_ss.at[half], recv_sem=c_rs.at[half],
            device_id=(pole, lower), device_id_type=MESH,
        )

    def core_copy(half, quad):
        start = 4 * quad + 2 * (1 - core)
        return pltpu.make_async_remote_copy(
            src_ref=terms.at[half, pl.ds(start, 2)], dst_ref=core_recv.at[half, quad],
            send_sem=q_ss.at[half, quad], recv_sem=q_rs.at[half, quad],
            device_id=core_mate, device_id_type=MESH,
        )

    def far_copy(half, quad):
        return pltpu.make_async_remote_copy(
            src_ref=core_recv.at[half, quad], dst_ref=far_recv.at[half],
            send_sem=y_ss.at[half], recv_sem=y_rs.at[half],
            device_id=side_mate, device_id_type=MESH,
        )

    def interface(half):
        last = dom == PARTS - 1
        t_next = jnp.where(last, 0.0, t_recv[half])
        below = first_s[half] - complex_rows(t_next, i_mat[1])
        c_send[half] = dot_nn(below.astype(BF16), u_mat[PB - 1])
        c_copy(half).start()
        above = jnp.where(last, 0.0, t_next - complex_rows(below, i_mat[2]))
        lifted_d[half] = dot_nt(above.astype(BF16), u_mat[PB - 1])

    def emit_terms(k, half):
        real_x = work[k, :H]
        imag_x = work[k, H:]
        terms[half, k, 0] = real_w * real_x - imag_w * imag_x
        terms[half, k, 1] = (
            real_wz * real_x - imag_wz * imag_x - real_w * f_half(k, half)
        )

    def second_solve(half):
        arrived = jnp.where(dom == 0, 0.0, c_recv[half])
        rows = jnp.concatenate([arrived[:H] + f_half(0, half), arrived[H:]], axis=0)
        work[0] = complex_rows(rows, g_mat[0])

        def forward(k, carry):
            work[k] = complex_rows(forward_step(k, half, False), g_mat[k])
            return carry

        lax.fori_loop(1, PB - 1, forward, 0)
        rows = forward_step(PB - 1, half, False) + lifted_d[half]
        work[PB - 1] = complex_rows(rows, g_mat[PB - 1])
        emit_terms(PB - 1, half)

        def backward(i, carry):
            k = PB - 2 - i
            lifted = dot_nt(work[k + 1].astype(BF16), u_mat[k])
            work[k] = work[k] + complex_rows(lifted, g_mat[k])
            emit_terms(k, half)
            return carry

        lax.fori_loop(0, 3, backward, 0)
        core_copy(half, 1).start()
        lax.fori_loop(3, PB - 1, backward, 0)
        core_copy(half, 0).start()

        for quad in (1, 0):
            core_copy(half, quad).wait()
            for i in range(2):
                core_recv[half, quad, i] += terms[half, 4 * quad + 2 * core + i]

            @pl.when(side == 1 - quad)
            def _():
                far_copy(half, quad).start()

    first_solve(0)
    pl.semaphore_wait(barrier, MATES)
    t_copy(0).start()
    interface_load.wait()
    wait_coupling(PB - 1)
    first_s[0] = complex_rows(work[PB - 1], i_mat[0])
    first_solve(1)
    t_copy(1).start()
    first_s[1] = complex_rows(work[PB - 1], i_mat[0])
    for half in range(2):
        t_copy(half).wait()
        interface(half)
    for half in range(2):
        c_copy(half).wait()
        second_solve(half)
    for half in range(2):
        far_copy(half, 0).wait()
        for i in range(2):
            y_ref[i, half * H : (half + 1) * H, :] = core_recv[half, side, i, 0] + far_recv[half, i, 0]
            z_own[i, half * H : (half + 1) * H, :] = core_recv[half, side, i, 1] + far_recv[half, i, 1]

    gram = exact_dot(y_ref[0], y_ref[0], 1, 1) + exact_dot(y_ref[1], y_ref[1], 1, 1)
    projected = exact_dot(y_ref[0], z_own[0], 1, 1) + exact_dot(y_ref[1], z_own[1], 1, 1)
    for i, part in enumerate((gram, projected)):
        parts[i, :M] = part[:, :H]
        parts[i, M:] = part[:, H:]

    def waited(ref, sem):
        pltpu.make_async_copy(ref, ref, sem).wait()

    swap = pltpu.make_async_remote_copy(
        src_ref=parts.at[1 - core], dst_ref=core_part, send_sem=a_ss.at[0], recv_sem=a_rs.at[0],
        device_id=core_mate, device_id_type=MESH,
    )
    swap.start()
    swap.wait()
    mine[...] = parts[core] + core_part[...]

    def scatter(step, carry):
        other, device = mate_of(step)
        pltpu.make_async_remote_copy(
            src_ref=mine.at[pl.ds(pl.multiple_of(other * PIECE, PIECE), PIECE)],
            dst_ref=pieces.at[step], send_sem=a_ss.at[1], recv_sem=a_rs.at[1],
            device_id=device, device_id_type=MESH,
        ).start()
        return carry

    lax.fori_loop(1, MATES, scatter, 0)
    own = pl.ds(pl.multiple_of(place * PIECE, PIECE), PIECE)
    waited(pieces.at[pl.ds(1, MATES - 1)], a_rs.at[1])
    waited(pieces.at[pl.ds(1, MATES - 1)], a_ss.at[1])
    pieces[0] = mine[own]
    sum_ref[core, own] = jnp.sum(pieces[...], axis=0) / (PARTS * PB * B)

    def gather(step, carry):
        pltpu.make_async_remote_copy(
            src_ref=sum_ref.at[core, own], dst_ref=sum_ref.at[core, own],
            send_sem=a_ss.at[2], recv_sem=a_rs.at[2],
            device_id=mate_of(step)[1], device_id_type=MESH,
        ).start()
        return carry

    lax.fori_loop(1, MATES, gather, 0)
    waited(pieces.at[pl.ds(1, MATES - 1)], a_rs.at[2])
    waited(pieces.at[pl.ds(1, MATES - 1)], a_ss.at[2])
    swap = pltpu.make_async_remote_copy(
        src_ref=sum_ref.at[core], dst_ref=sum_ref.at[core],
        send_sem=a_ss.at[3], recv_sem=a_rs.at[3],
        device_id=core_mate, device_id_type=MESH,
    )
    swap.start()
    swap.wait()


def filtered_sums(f, u, g, interface, pole_values):
    own = jax.ShapeDtypeStruct((2, M, B), F32)
    dma = pltpu.SemaphoreType.DMA
    return pl.pallas_call(
        filter_kernel,
        out_shape=(own, jax.ShapeDtypeStruct((2, 2 * M, H), F32)),
        in_specs=[pl.BlockSpec(memory_space=pl.ANY)] * 4 + [pl.BlockSpec(memory_space=pltpu.SMEM)],
        out_specs=(pl.BlockSpec(memory_space=pltpu.VMEM), pl.BlockSpec(memory_space=pltpu.VMEM)),
        scratch_shapes=[
            pltpu.VMEM((PB, B, M), BF16),
            pltpu.VMEM((PB, M, B), BF16),
            pltpu.VMEM((PB, B, B), BF16),
            pltpu.VMEM((PB, 2 * B, B), BF16),
            pltpu.VMEM((3, 2 * B, B), BF16),
            pltpu.VMEM((PB, M, B), F32),
            pltpu.VMEM((2, M, B), F32),
            pltpu.VMEM((2, M, B), F32),
            pltpu.VMEM((2, M, B), F32),
            pltpu.VMEM((2, M, B), F32),
            pltpu.VMEM((2, M, B), F32),
            pltpu.VMEM((2, M, B), F32),
            pltpu.VMEM((2, PB, 2, H, B), F32),
            pltpu.VMEM((2, 2, 2, 2, H, B), F32),
            pltpu.VMEM((2, 2, 2, H, B), F32),
            pltpu.VMEM((2, M, B), F32),
            pltpu.VMEM((2, 2 * M, H), F32),
            pltpu.VMEM((2 * M, H), F32),
            pltpu.VMEM((2 * M, H), F32),
            pltpu.VMEM((MATES, PIECE, H), F32),
            dma((PB,)), dma((PB,)), dma((PB,)), dma,
            dma((2,)), dma((2,)), dma((2,)), dma((2,)),
            dma((2, 2)), dma((2, 2)), dma((2,)), dma((2,)), dma((4,)), dma((4,)),
        ],
        compiler_params=pltpu.CompilerParams(
            collective_id=0, has_side_effects=True, vmem_limit_bytes=60 * 2**20
        ),
        name="filter_sums",
    )(f, u, g, interface, pole_values)


def factor_block(block, inverse):
    shape = (8, 2 * NB)
    groups = NB // 8
    row = lax.broadcasted_iota(jnp.int32, (NB, NB), 0)
    column = lax.broadcasted_iota(jnp.int32, (NB, NB), 1)
    start = jnp.concatenate([block, jnp.where(row == column, 1.0, 0.0)], axis=1)
    place = lax.broadcasted_iota(jnp.int32, shape, 0)
    rows = [start[8 * g : 8 * g + 8, :] for g in range(groups)]
    scales = [jnp.zeros(shape, F32) for g in range(groups)]
    for first in range(0, NB, SPAN):
        spread = {
            (g, j): jnp.broadcast_to(rows[g][:, first + j : first + j + 1], shape)
            for g in range(first // 8, groups)
            for j in range(SPAN)
        }
        for j in range(SPAN):
            pivot, at = divmod(first + j, 8)
            scale = 1.0 / jnp.broadcast_to(spread[pivot, j][at : at + 1], shape)
            scales[pivot] = jnp.where(place == at, scale, scales[pivot])
            pivot_row = jnp.broadcast_to(rows[pivot][at : at + 1], shape) * scale
            rest = range(j + 1, SPAN)
            across = [jnp.broadcast_to(spread[pivot, i][at : at + 1], shape) * scale for i in rest]
            for g in range(pivot, groups):
                taken = spread[g, j]
                if g == pivot:
                    taken = jnp.where(place > at, taken, 0.0)
                rows[g] = rows[g] - taken * pivot_row
                for i, value in zip(rest, across):
                    spread[g, i] = spread[g, i] - taken * value
    for g in range(groups):
        inverse[8 * g : 8 * g + 8, :] = rows[g] * jnp.sqrt(scales[g])


def basis_kernel(sum_ref, y_ref, basis_ref, rayleigh_ref, wide, block, inverse):
    row = lax.broadcasted_iota(jnp.int32, (M, M), 0)
    column = lax.broadcasted_iota(jnp.int32, (M, M), 1)
    wide[:, :H] = sum_ref[0, :M]
    wide[:, H:M] = sum_ref[0, M:]
    wide[:, M:] = jnp.where(row == column, 1.0, 0.0)
    for low in range(0, M, NB):
        high = low + NB
        factor_block(wide[low:high, low:high], block)
        reduced = exact_dot(block[:, NB:], wide[low:high, :], 1, 0)
        inverse[low:high, :] = reduced[:, M:]
        if high < M:
            change = exact_dot(reduced[:, :M], reduced, 0, 0)
            wide[high:, :] = wide[high:, :] - change[high:]
    projected = jnp.concatenate([sum_ref[1, :M], sum_ref[1, M:]], axis=1)
    middle = exact_dot(inverse[...], projected, 1, 0)
    rayleigh_ref[...] = exact_dot(middle, inverse[...], 1, 1)
    for i in range(2):
        basis_ref[i] = exact_dot(inverse[...], y_ref[i], 1, 0).T


def orthonormal_basis(sums, y_rows):
    return pl.pallas_call(
        basis_kernel,
        out_shape=(
            jax.ShapeDtypeStruct((2, B, M), F32),
            jax.ShapeDtypeStruct((M, M), F32),
        ),
        in_specs=[pl.BlockSpec(memory_space=pltpu.VMEM)] * 2,
        out_specs=(pl.BlockSpec(memory_space=pltpu.VMEM), pl.BlockSpec(memory_space=pltpu.VMEM)),
        scratch_shapes=[
            pltpu.VMEM((M, 2 * M), F32),
            pltpu.VMEM((NB, 2 * NB), F32),
            pltpu.VMEM((M, M), F32),
        ],
        compiler_params=pltpu.CompilerParams(vmem_limit_bytes=32 * 2**20),
        name="orthonormal_basis",
    )(sums, y_rows)


def on_device(initial_block, coupling, pivots, interface, pole_values):
    y_rows, sums = filtered_sums(
        initial_block[0],
        coupling[0],
        pivots[0, 0].reshape(PB, 2 * B, B),
        interface[0, 0].reshape(3, 2 * B, B),
        pole_values,
    )
    basis, rayleigh = orthonormal_basis(sums, y_rows)
    return (basis[None], rayleigh)


def solution(mesh):
    in_specs = (
        P("dom", None, None, None),
        P("dom", None, None, None),
        P("pole", "dom", None, None, None, None),
        P("pole", "dom", None, None, None, None),
        P("pole", None),
    )
    out_specs = (P("dom", "pole", None, None), P())
    return jax.shard_map(
        on_device, mesh=mesh, in_specs=in_specs, out_specs=out_specs, check_vma=False
    )
```

```python
import jax
import jax.numpy as jnp
from jax import lax
from jax.experimental import pallas as pl
from jax.experimental.pallas import tpu as pltpu
from jax.sharding import PartitionSpec as P

B = 512
M = 256
H = M // 2
PB = 8
PARTS = 32
F32 = jnp.float32
BF16 = jnp.bfloat16
MESH = pl.DeviceIdType.MESH
HIGHEST = lax.Precision.HIGHEST
MATES = 2 * PARTS
PIECE = 2 * M // MATES
NB = 64
SPAN = 16


def dot_nn(left, right):
    return jnp.dot(left, right, preferred_element_type=F32)


def dot_nt(left, right):
    return lax.dot_general(left, right, (((1,), (1,)), ((), ())), preferred_element_type=F32)


def exact_dot(left, right, left_dim, right_dim):
    return lax.dot_general(
        left, right, (((left_dim,), (right_dim,)), ((), ())),
        precision=HIGHEST, preferred_element_type=F32,
    )


def complex_rows(rows, matrix):
    out = dot_nt(rows.astype(BF16), matrix)
    real_part = out[:H, :B] - out[H:, B:]
    imag_part = out[H:, :B] + out[:H, B:]
    return jnp.concatenate([real_part, imag_part], axis=0)


def filter_kernel(
    f_hbm, u_hbm, g_hbm, i_hbm, pole_ref, y_ref, sum_ref,
    f_raw, f_rows, u_mat, g_mat, i_mat, work, first_s, lifted_d,
    t_send, t_recv, c_send, c_recv, terms, core_recv, far_recv,
    z_own, parts, core_part, mine, pieces,
    f_sem, u_sem, g_sem, i_sem, t_ss, t_rs, c_ss, c_rs, q_ss, q_rs, y_ss, y_rs, a_ss, a_rs,
):
    pole = lax.axis_index("pole")
    dom = lax.axis_index("dom")
    core = lax.rem(pole, 2)
    side = pole // 2
    upper = lax.rem(dom + PARTS - 1, PARTS)
    lower = lax.rem(dom + 1, PARTS)
    core_mate = (2 * side + 1 - core, dom)
    side_mate = (2 * (1 - side) + core, dom)

    loads = []
    for k in range(PB):
        loads.append(
            (
                pltpu.make_async_copy(f_hbm.at[k], f_raw.at[k], f_sem.at[k]),
                pltpu.make_async_copy(g_hbm.at[k], g_mat.at[k], g_sem.at[k]),
                pltpu.make_async_copy(u_hbm.at[k], u_mat.at[k], u_sem.at[k]),
            )
        )
        for copy in loads[-1]:
            copy.start()
    interface_load = pltpu.make_async_copy(i_hbm, i_mat, i_sem)
    interface_load.start()

    barrier = pltpu.get_barrier_semaphore()
    place = side * PARTS + dom

    def mate_of(step):
        other = lax.rem(place + step, MATES)
        return other, (2 * (other // PARTS) + core, lax.rem(other, PARTS))

    pl.semaphore_signal(barrier, inc=1, device_id=core_mate, device_id_type=MESH)

    def greet(step, carry):
        pl.semaphore_signal(barrier, inc=1, device_id=mate_of(step)[1], device_id_type=MESH)
        return carry

    lax.fori_loop(1, MATES, greet, 0)

    real_z = pole_ref[0, 0]
    imag_z = pole_ref[0, 1]
    real_w = pole_ref[0, 2]
    imag_w = pole_ref[0, 3]
    real_wz = real_w * real_z - imag_w * imag_z
    imag_wz = real_w * imag_z + imag_w * real_z

    def f_half(k, half):
        return f_rows[k, half * H : (half + 1) * H, :].astype(F32)

    def wait_load(k):
        pltpu.make_async_copy(f_hbm.at[k], f_raw.at[k], f_sem.at[k]).wait()
        pltpu.make_async_copy(g_hbm.at[k], g_mat.at[k], g_sem.at[k]).wait()
        f_rows[k] = f_raw[k].T

    def wait_coupling(k):
        pltpu.make_async_copy(u_hbm.at[k], u_mat.at[k], u_sem.at[k]).wait()

    def forward_step(k, half, loading):
        if loading:
            wait_load(k)
            wait_coupling(k - 1)
        lifted = dot_nn(work[k - 1].astype(BF16), u_mat[k - 1])
        rows = jnp.concatenate([lifted[:H] + f_half(k, half), lifted[H:]], axis=0)
        return rows

    def first_solve(half):
        loading = half == 0
        if loading:
            wait_load(0)
        out = dot_nt(f_rows[0, half * H : (half + 1) * H, :], g_mat[0])
        work[0] = jnp.concatenate([out[:, :B], out[:, B:]], axis=0)

        def forward(k, carry):
            work[k] = complex_rows(forward_step(k, half, loading), g_mat[k])
            return carry

        lax.fori_loop(1, PB, forward, 0)

        def backward(i, carry):
            k = PB - 2 - i
            lifted = dot_nt(work[k + 1].astype(BF16), u_mat[k])
            work[k] = work[k] + complex_rows(lifted, g_mat[k])
            return carry

        lax.fori_loop(0, PB - 1, backward, 0)
        t_send[half] = work[0]

    def t_copy(half):
        return pltpu.make_async_remote_copy(
            src_ref=t_send.at[half], dst_ref=t_recv.at[half],
            send_sem=t_ss.at[half], recv_sem=t_rs.at[half],
            device_id=(pole, upper), device_id_type=MESH,
        )

    def c_copy(half):
        return pltpu.make_async_remote_copy(
            src_ref=c_send.at[half], dst_ref=c_recv.at[half],
            send_sem=c_ss.at[half], recv_sem=c_rs.at[half],
            device_id=(pole, lower), device_id_type=MESH,
        )

    def core_copy(half, quad, i):
        return pltpu.make_async_remote_copy(
            src_ref=terms.at[half, 4 * quad + 2 * (1 - core) + i],
            dst_ref=core_recv.at[half, quad, i],
            send_sem=q_ss.at[half, quad, i], recv_sem=q_rs.at[half, quad, i],
            device_id=core_mate, device_id_type=MESH,
        )

    def far_copy(half, i, kind):
        return pltpu.make_async_remote_copy(
            src_ref=core_recv.at[half, 1 - side, i, kind], dst_ref=far_recv.at[half, i, kind],
            send_sem=y_ss.at[half, i, kind], recv_sem=y_rs.at[half, i, kind],
            device_id=side_mate, device_id_type=MESH,
        )

    def far_sum(half, i, kind):
        far_copy(half, i, kind).wait()
        target = (y_ref, z_own)[kind]
        target[i, half * H : (half + 1) * H, :] = (
            core_recv[half, side, i, kind] + far_recv[half, i, kind]
        )

    def interface(half):
        last = dom == PARTS - 1
        t_next = jnp.where(last, 0.0, t_recv[half])
        below = first_s[half] - complex_rows(t_next, i_mat[1])
        c_send[half] = dot_nn(below.astype(BF16), u_mat[PB - 1])
        c_copy(half).start()
        above = jnp.where(last, 0.0, t_next - complex_rows(below, i_mat[2]))
        lifted_d[half] = dot_nt(above.astype(BF16), u_mat[PB - 1])

    def emit_terms(k, half):
        real_x = work[k, :H]
        imag_x = work[k, H:]
        terms[half, k, 0] = real_w * real_x - imag_w * imag_x
        terms[half, k, 1] = (
            real_wz * real_x - imag_wz * imag_x - real_w * f_half(k, half)
        )

    def second_solve(half):
        arrived = jnp.where(dom == 0, 0.0, c_recv[half])
        rows = jnp.concatenate([arrived[:H] + f_half(0, half), arrived[H:]], axis=0)
        work[0] = complex_rows(rows, g_mat[0])

        def forward(k, carry):
            work[k] = complex_rows(forward_step(k, half, False), g_mat[k])
            return carry

        lax.fori_loop(1, PB - 1, forward, 0)
        rows = forward_step(PB - 1, half, False) + lifted_d[half]
        work[PB - 1] = complex_rows(rows, g_mat[PB - 1])
        emit_terms(PB - 1, half)

        def backward(i, carry):
            k = PB - 2 - i
            lifted = dot_nt(work[k + 1].astype(BF16), u_mat[k])
            work[k] = work[k] + complex_rows(lifted, g_mat[k])
            emit_terms(k, half)
            return carry

        lax.fori_loop(0, 3, backward, 0)
        for i in (1, 0):
            core_copy(half, 1, i).start()
        lax.fori_loop(3, PB - 1, backward, 0)
        for i in (1, 0):
            core_copy(half, 0, i).start()

        for quad in (1, 0):
            for i in (1, 0):
                core_copy(half, quad, i).wait()
                core_recv[half, quad, i] += terms[half, 4 * quad + 2 * core + i]

                @pl.when(side == 1 - quad)
                def _():
                    for kind in range(2):
                        far_copy(half, i, kind).start()

    first_solve(0)
    pl.semaphore_wait(barrier, MATES)
    t_copy(0).start()
    interface_load.wait()
    wait_coupling(PB - 1)
    first_s[0] = complex_rows(work[PB - 1], i_mat[0])
    first_solve(1)
    t_copy(1).start()
    first_s[1] = complex_rows(work[PB - 1], i_mat[0])
    for half in range(2):
        t_copy(half).wait()
        interface(half)
    for half in range(2):
        c_copy(half).wait()
        second_solve(half)
    for i in (1, 0):
        for kind in range(2):
            far_sum(0, i, kind)
    for i in (1, 0):
        for kind in range(2):
            far_sum(1, i, kind)
            product = exact_dot(y_ref[i], (y_ref, z_own)[kind][i], 1, 1)
            if i == 1:
                parts[kind, :M] = product[:, :H]
                parts[kind, M:] = product[:, H:]
            else:
                parts[kind, :M] += product[:, :H]
                parts[kind, M:] += product[:, H:]

    def waited(ref, sem):
        pltpu.make_async_copy(ref, ref, sem).wait()

    swap = pltpu.make_async_remote_copy(
        src_ref=parts.at[1 - core], dst_ref=core_part, send_sem=a_ss.at[0], recv_sem=a_rs.at[0],
        device_id=core_mate, device_id_type=MESH,
    )
    swap.start()
    swap.wait()
    mine[...] = parts[core] + core_part[...]

    def scatter(step, carry):
        other, device = mate_of(step)
        pltpu.make_async_remote_copy(
            src_ref=mine.at[pl.ds(pl.multiple_of(other * PIECE, PIECE), PIECE)],
            dst_ref=pieces.at[step], send_sem=a_ss.at[1], recv_sem=a_rs.at[1],
            device_id=device, device_id_type=MESH,
        ).start()
        return carry

    lax.fori_loop(1, MATES, scatter, 0)
    own = pl.ds(pl.multiple_of(place * PIECE, PIECE), PIECE)
    waited(pieces.at[pl.ds(1, MATES - 1)], a_rs.at[1])
    waited(pieces.at[pl.ds(1, MATES - 1)], a_ss.at[1])
    pieces[0] = mine[own]
    sum_ref[core, own] = jnp.sum(pieces[...], axis=0) / (PARTS * PB * B)

    def gather(step, carry):
        pltpu.make_async_remote_copy(
            src_ref=sum_ref.at[core, own], dst_ref=sum_ref.at[core, own],
            send_sem=a_ss.at[2], recv_sem=a_rs.at[2],
            device_id=mate_of(step)[1], device_id_type=MESH,
        ).start()
        return carry

    lax.fori_loop(1, MATES, gather, 0)
    waited(pieces.at[pl.ds(1, MATES - 1)], a_rs.at[2])
    waited(pieces.at[pl.ds(1, MATES - 1)], a_ss.at[2])
    swap = pltpu.make_async_remote_copy(
        src_ref=sum_ref.at[core], dst_ref=sum_ref.at[core],
        send_sem=a_ss.at[3], recv_sem=a_rs.at[3],
        device_id=core_mate, device_id_type=MESH,
    )
    swap.start()
    swap.wait()


def filtered_sums(f, u, g, interface, pole_values):
    own = jax.ShapeDtypeStruct((2, M, B), F32)
    dma = pltpu.SemaphoreType.DMA
    return pl.pallas_call(
        filter_kernel,
        out_shape=(own, jax.ShapeDtypeStruct((2, 2 * M, H), F32)),
        in_specs=[pl.BlockSpec(memory_space=pl.ANY)] * 4 + [pl.BlockSpec(memory_space=pltpu.SMEM)],
        out_specs=(pl.BlockSpec(memory_space=pltpu.VMEM), pl.BlockSpec(memory_space=pltpu.VMEM)),
        scratch_shapes=[
            pltpu.VMEM((PB, B, M), BF16),
            pltpu.VMEM((PB, M, B), BF16),
            pltpu.VMEM((PB, B, B), BF16),
            pltpu.VMEM((PB, 2 * B, B), BF16),
            pltpu.VMEM((3, 2 * B, B), BF16),
            pltpu.VMEM((PB, M, B), F32),
            pltpu.VMEM((2, M, B), F32),
            pltpu.VMEM((2, M, B), F32),
            pltpu.VMEM((2, M, B), F32),
            pltpu.VMEM((2, M, B), F32),
            pltpu.VMEM((2, M, B), F32),
            pltpu.VMEM((2, M, B), F32),
            pltpu.VMEM((2, PB, 2, H, B), F32),
            pltpu.VMEM((2, 2, 2, 2, H, B), F32),
            pltpu.VMEM((2, 2, 2, H, B), F32),
            pltpu.VMEM((2, M, B), F32),
            pltpu.VMEM((2, 2 * M, H), F32),
            pltpu.VMEM((2 * M, H), F32),
            pltpu.VMEM((2 * M, H), F32),
            pltpu.VMEM((MATES, PIECE, H), F32),
            dma((PB,)), dma((PB,)), dma((PB,)), dma,
            dma((2,)), dma((2,)), dma((2,)), dma((2,)),
            dma((2, 2, 2)), dma((2, 2, 2)), dma((2, 2, 2)), dma((2, 2, 2)), dma((4,)), dma((4,)),
        ],
        compiler_params=pltpu.CompilerParams(
            collective_id=0, has_side_effects=True, vmem_limit_bytes=60 * 2**20
        ),
        name="filter_sums",
    )(f, u, g, interface, pole_values)


def factor_block(block, inverse):
    shape = (8, 2 * NB)
    groups = NB // 8
    row = lax.broadcasted_iota(jnp.int32, (NB, NB), 0)
    column = lax.broadcasted_iota(jnp.int32, (NB, NB), 1)
    start = jnp.concatenate([block, jnp.where(row == column, 1.0, 0.0)], axis=1)
    place = lax.broadcasted_iota(jnp.int32, shape, 0)
    rows = [start[8 * g : 8 * g + 8, :] for g in range(groups)]
    scales = [jnp.zeros(shape, F32) for g in range(groups)]
    for first in range(0, NB, SPAN):
        spread = {
            (g, j): jnp.broadcast_to(rows[g][:, first + j : first + j + 1], shape)
            for g in range(first // 8, groups)
            for j in range(SPAN)
        }
        for j in range(SPAN):
            pivot, at = divmod(first + j, 8)
            scale = 1.0 / jnp.broadcast_to(spread[pivot, j][at : at + 1], shape)
            scales[pivot] = jnp.where(place == at, scale, scales[pivot])
            pivot_row = jnp.broadcast_to(rows[pivot][at : at + 1], shape) * scale
            rest = range(j + 1, SPAN)
            across = [jnp.broadcast_to(spread[pivot, i][at : at + 1], shape) * scale for i in rest]
            for g in range(pivot, groups):
                taken = spread[g, j]
                if g == pivot:
                    taken = jnp.where(place > at, taken, 0.0)
                rows[g] = rows[g] - taken * pivot_row
                for i, value in zip(rest, across):
                    spread[g, i] = spread[g, i] - taken * value
    for g in range(groups):
        inverse[8 * g : 8 * g + 8, :] = rows[g] * jnp.sqrt(scales[g])


def basis_kernel(sum_ref, y_hbm, basis_ref, rayleigh_ref, wide, block, inverse, y_ref, y_sem):
    load = pltpu.make_async_copy(y_hbm, y_ref, y_sem)
    load.start()
    row = lax.broadcasted_iota(jnp.int32, (M, M), 0)
    column = lax.broadcasted_iota(jnp.int32, (M, M), 1)
    wide[:, :H] = sum_ref[0, :M]
    wide[:, H:M] = sum_ref[0, M:]
    wide[:, M:] = jnp.where(row == column, 1.0, 0.0)
    for low in range(0, M, NB):
        high = low + NB
        factor_block(wide[low:high, low:high], block)
        reduced = exact_dot(block[:, NB:], wide[low:high, :], 1, 0)
        inverse[low:high, :] = reduced[:, M:]
        if high < M:
            change = exact_dot(reduced[:, :M], reduced, 0, 0)
            wide[high:, :] = wide[high:, :] - change[high:]
    projected = jnp.concatenate([sum_ref[1, :M], sum_ref[1, M:]], axis=1)
    middle = exact_dot(inverse[...], projected, 1, 0)
    rayleigh_ref[...] = exact_dot(middle, inverse[...], 1, 1)
    load.wait()
    for i in range(2):
        basis_ref[i] = exact_dot(inverse[...], y_ref[i], 1, 0).T


def orthonormal_basis(sums, y_rows):
    return pl.pallas_call(
        basis_kernel,
        out_shape=(
            jax.ShapeDtypeStruct((2, B, M), F32),
            jax.ShapeDtypeStruct((M, M), F32),
        ),
        in_specs=[pl.BlockSpec(memory_space=pltpu.VMEM), pl.BlockSpec(memory_space=pl.ANY)],
        out_specs=(pl.BlockSpec(memory_space=pltpu.VMEM), pl.BlockSpec(memory_space=pltpu.VMEM)),
        scratch_shapes=[
            pltpu.VMEM((M, 2 * M), F32),
            pltpu.VMEM((NB, 2 * NB), F32),
            pltpu.VMEM((M, M), F32),
            pltpu.VMEM((2, M, B), F32),
            pltpu.SemaphoreType.DMA,
        ],
        compiler_params=pltpu.CompilerParams(vmem_limit_bytes=60 * 2**20),
        name="orthonormal_basis",
    )(sums, y_rows)


def on_device(initial_block, coupling, pivots, interface, pole_values):
    y_rows, sums = filtered_sums(
        initial_block[0],
        coupling[0],
        pivots[0, 0].reshape(PB, 2 * B, B),
        interface[0, 0].reshape(3, 2 * B, B),
        pole_values,
    )
    basis, rayleigh = orthonormal_basis(sums, y_rows)
    return (basis[None], rayleigh)


def solution(mesh):
    in_specs = (
        P("dom", None, None, None),
        P("dom", None, None, None),
        P("pole", "dom", None, None, None, None),
        P("pole", "dom", None, None, None, None),
        P("pole", None),
    )
    out_specs = (P("dom", "pole", None, None), P())
    return jax.shard_map(
        on_device, mesh=mesh, in_specs=in_specs, out_specs=out_specs, check_vma=False
    )
```
